32 devices in a mesh: parts: 2 (over x), sec: 16 (over z, y, core).
Axes of the slice: x: 2, y: 2, z: 4, core: 2. Of those that a mesh axis runs over, the one named last changes fastest.
Arguments:
- wave_blocks: bfloat16 [32, 2, 128, 128], P(('parts', 'sec')), parts along dimension 0, may hold values from -6 to 6
- slot_sector: int32 [32], P('parts'), parts along dimension 0, may hold values from 0 to 15, each once
- sector_rows: int32 [32], P('parts'), parts along dimension 0, may hold values from 32 to 128
- sector_cols: int32 [32], P('parts'), parts along dimension 0, may hold values from 32 to 128
- left_ops: bfloat16 [256, 128, 128], P(('parts', 'sec')), parts along dimension 0, may hold values from -0.5 to 0.5
- right_ops: bfloat16 [256, 128, 128], P(('parts', 'sec')), parts along dimension 0, may hold values from -0.5 to 0.5
- term_coef: float32 [256, 16], P(('parts', 'sec')), parts along dimension 0, may hold values from -1.25 to 1.25
- term_shift: int32 [256], P(('parts', 'sec')), parts along dimension 0, may hold values from -2 to 2
Outputs:
- sigma_blocks: bfloat16 [32, 2, 128, 128], P(('parts', 'sec')), parts along dimension 0
The draws below stay inside these ranges and needn't reach their ends.
There are 2 independent parts, one for each index of `parts`. The reference program is written for one: setup_inputs(seed, part) draws one part's arguments, and reference() takes and returns one part's arrays. A program takes and returns all parts, laid end to end along the dimension named above; each array names one. Nothing has to cross between parts.
Inputs may be any that keep to these rules, and one draw needn't show every extreme that they name: slot_sector holds each label 0 .. 15 exactly once.
All inputs are finite; a program needn't handle non-finite values.
Results may differ from the reference program's by a relative error of at most 0.0049.
Values may be sent and summed in bfloat16 or wider, within the bound.
A program may use at most 128 MiB of HBM per device.

```python
import jax
import jax.numpy as jnp
from jax import lax

BL = 128
BR = 128
SECTORS = 16
NTERMS = 128


def set_ends(drawn, rng, low, largest):
    spot = [jax.random.randint(jax.random.fold_in(rng, axis), (), 0, length) for axis, length in enumerate(drawn.shape)]
    widest = drawn.shape.index(max(drawn.shape))
    next_to = spot[:widest] + [(spot[widest] + 1) % drawn.shape[widest]] + spot[widest + 1:]
    return drawn.at[tuple(spot)].set(low).at[tuple(next_to)].set(largest)


def shard_levels(own_key, dims, cuts, least, high):
    loudness, own = 1.0, jax.random.fold_in(own_key, 6)
    for dim, shards_of in cuts:
        heights = jnp.exp(jax.random.uniform(jax.random.fold_in(own, dim), (shards_of,), jnp.float32, least / len(cuts), high / len(cuts)))
        loudness = loudness * jnp.repeat(heights, dims[dim] // shards_of).reshape([-1 if axis == dim else 1 for axis in range(len(dims))])
    return loudness


def normal_values(stream_key, extent, width, limit, cuts=(), held_as=jnp.bfloat16):
    result = width * jax.random.normal(stream_key, extent, jnp.float32)
    if cuts:
        result = result * shard_levels(stream_key, extent, cuts, -0.22, 0.18)
    return jnp.clip(result, -limit, limit).astype(held_as)


def setup_inputs(seed: int = 0, part: int = 0) -> dict:
    key_list = jax.random.split(jax.random.key(seed), 9)
    part_keys = jax.random.split(jax.random.fold_in(key_list[8], part), 9)
    wave_blocks = normal_values(part_keys[0], (SECTORS, 2, BL, BR), 1.0, 6.0, ((0, 16),))
    slot_sector = jax.random.permutation(part_keys[1], SECTORS).astype(jnp.int32)
    sector_rows = set_ends(jax.random.randint(part_keys[2], (SECTORS,), BL // 4, BL + 1), jax.random.fold_in(part_keys[2], 1), BL // 4, BL).astype(jnp.int32)
    sector_cols = set_ends(jax.random.randint(part_keys[3], (SECTORS,), BR // 4, BR + 1), jax.random.fold_in(part_keys[3], 1), BR // 4, BR).astype(jnp.int32)
    left_ops = normal_values(part_keys[4], (NTERMS, BL, BL), BL ** -0.5, 0.5, ((0, 16),))
    right_ops = normal_values(part_keys[5], (NTERMS, BR, BR), BR ** -0.5, 0.5, ((0, 16),))
    term_coef = normal_values(part_keys[6], (NTERMS, SECTORS), (NTERMS ** -0.5), 1.25, ((0, 16),), jnp.float32)
    term_shift = set_ends(jax.random.randint(part_keys[7], (NTERMS,), -2, 3), jax.random.fold_in(part_keys[7], 1), -2, 2).astype(jnp.int32)
    return {"wave_blocks": wave_blocks, "slot_sector": slot_sector, "sector_rows": sector_rows, "sector_cols": sector_cols, "left_ops": left_ops, "right_ops": right_ops, "term_coef": term_coef, "term_shift": term_shift}


max_shift = 2


def live_cells(labels, sector_rows, sector_cols, left_size, right_size):
    row_live = jnp.arange(left_size, dtype=jnp.int32)[None, :] < sector_rows[labels][:, None]
    col_live = jnp.arange(right_size, dtype=jnp.int32)[None, :] < sector_cols[labels][:, None]
    return (row_live[:, :, None] & col_live[:, None, :])[:, None]


def reference(wave_blocks, slot_sector, sector_rows, sector_cols, left_ops, right_ops, term_coef, term_shift):
    everything = jnp.arange(SECTORS, dtype=jnp.int32)
    inverse = jnp.zeros((SECTORS,), jnp.int32).at[slot_sector].set(everything)
    live_mask = live_cells(everything, sector_rows, sector_cols, BL, BR)
    states = jnp.where(live_mask, wave_blocks[inverse], jnp.zeros((), wave_blocks.dtype))
    padded = jnp.pad(states, ((max_shift, max_shift), (0, 0), (0, 0), (0, 0)))

    def add_term(summed, term_pack):
        left_op, right_op, coeff_row, shift_term = term_pack
        begin = (max_shift - shift_term).astype(jnp.int32)
        source = lax.dynamic_slice_in_dim(padded, begin, SECTORS, 0)
        halfway = jnp.einsum("ab,svbc->svac", left_op.astype(jnp.float32), source.astype(jnp.float32)).astype(jnp.bfloat16)
        product_term = jnp.einsum("svac,cd->svad", halfway.astype(jnp.float32), right_op.astype(jnp.float32))
        return summed + coeff_row[:, None, None, None] * product_term, None

    start_sum = jnp.zeros((SECTORS, 2, BL, BR), jnp.float32)
    summed, unused = lax.scan(add_term, start_sum, (left_ops, right_ops, term_coef, term_shift))
    masked_sum = jnp.where(live_mask, summed, jnp.zeros((), jnp.float32)).astype(jnp.bfloat16)
    return masked_sum[slot_sector]
```

```python
import functools

import jax
import jax.numpy as jnp
from jax import lax
from jax.experimental import pallas as pl
from jax.experimental.pallas import tpu as pltpu
from jax.sharding import PartitionSpec as P

MESH = pl.DeviceIdType.MESH
REACH = 2


def sigma_kernel(
    n, wave, slots, rows, cols, left, right, coef, shift, coef_far, shift_far,
    out,
    lefts, rights, coef_b, shift_b, coef_in, shift_in, states, half, inverse,
    part_out, part_in, sum_out, sum_in,
    local_sem, ops_send, ops_recv, z_send, z_recv, y_send, y_recv,
    part_send, part_recv, sum_send, sum_recv,
):
    depth = n // 4

    def repeat(begin, end, body, carry):
        if depth > 4:
            return lax.fori_loop(begin, end, body, carry)
        for step in range(begin, end):
            carry = body(step, carry)
        return carry

    terms = left.shape[0]
    size = wave.shape[2]
    me = lax.axis_index("sec")
    core = lax.rem(me, 2)
    y = lax.rem(me // 2, 2)
    z = me // 4

    def core_at(which):
        return 1 - core if which else core

    def row_to(step):
        return lax.rem(z + step, depth)

    def place(step, column, which):
        return (step * 2 + column) * 2 + which

    def slot_of(row, column, which):
        return (row * 2 + (1 - y if column else y)) * 2 + core_at(which)

    def slot_from(step, column, which):
        return slot_of(lax.rem(z + depth - step, depth), column, which)

    def device(row, column, which):
        return {"sec": slot_of(row, column, which)}

    def remote(src, dst, send, recv, target):
        return pltpu.make_async_remote_copy(
            src_ref=src, dst_ref=dst, send_sem=send, recv_sem=recv, device_id=target, device_id_type=MESH
        )

    local = [
        pltpu.make_async_copy(wave.at[0, core], states.at[0], local_sem.at[0]),
        pltpu.make_async_copy(left, lefts.at[pl.ds(0, terms)], local_sem.at[1]),
        pltpu.make_async_copy(right, rights.at[pl.ds(0, terms)], local_sem.at[2]),
    ]
    for copy in local:
        copy.start()

    barrier = pltpu.get_barrier_semaphore()

    def greet(step, carry):
        for which in range(2):
            pl.semaphore_signal(barrier, inc=1, device_id=device(row_to(step), 0, which), device_id_type=MESH)
        return carry

    partner = device(z, 0, 1)
    neighbour = device(z, 1, 0)
    pl.semaphore_signal(barrier, inc=1, device_id=partner, device_id_type=MESH)
    pl.semaphore_signal(barrier, inc=1, device_id=neighbour, device_id_type=MESH)
    repeat(1, depth, greet, 0)
    pl.semaphore_wait(barrier, 2 * depth)

    def z_copy(step, which):
        at = step * 2 + which
        return remote(
            wave.at[0, core_at(which)], states.at[place(step, 0, which)], z_send.at[at], z_recv.at[at],
            device(row_to(step), 0, which),
        )

    def y_copy(step, which):
        at = step * 2 + which
        return remote(
            states.at[place(step, 0, which)], states.at[place(step, 1, which)], y_send.at[at], y_recv.at[at],
            neighbour,
        )

    others = [
        remote(shift_far, shift_in, ops_send.at[0], ops_recv.at[0], partner),
        remote(coef_far, coef_in, ops_send.at[1], ops_recv.at[1], partner),
        remote(left, lefts.at[pl.ds(terms, terms)], ops_send.at[2], ops_recv.at[2], partner),
        remote(right, rights.at[pl.ds(terms, terms)], ops_send.at[3], ops_recv.at[3], partner),
    ]

    def send_column(step, carry):
        for which in range(2):
            z_copy(step, which).start()
        return carry

    repeat(1, depth, send_column, 0)
    z_copy(0, 1).start()
    for copy in others[:3]:
        copy.start()
    local[0].wait()
    y_copy(0, 0).start()
    others[3].start()

    for label in range(REACH):
        inverse[label] = n
        inverse[n + REACH + label] = n

    def slot_at(at):
        row = lax.rem(z + depth - at // 4, depth)
        column = lax.rem(y + lax.rem(at // 2, 2), 2)
        return (row * 2 + column) * 2 + lax.rem(core + lax.rem(at, 2), 2)

    def invert(label, carry):
        found = lax.fori_loop(
            0, n, lambda slot, seen: jnp.maximum(seen, jnp.where(slots[slot_at(slot)] == label, slot, 0)), jnp.int32(0)
        )
        inverse[label + REACH] = found
        return carry

    lax.fori_loop(0, n, invert, 0)

    def clear(term, carry):
        half[n, term] = jnp.zeros((size, size), half.dtype)
        return carry

    lax.fori_loop(0, 2 * terms, clear, 0)

    row_of = lax.broadcasted_iota(jnp.int32, (size, size), 0)
    col_of = lax.broadcasted_iota(jnp.int32, (size, size), 1)

    def live(slot):
        label = slots[slot]
        return (row_of < rows[label]) & (col_of < cols[label])

    def weight(term, slot):
        moved = slots[slot]
        if term < terms:
            return coef[term, jnp.clip(moved + shift[term], 0, n - 1)]
        return coef_b[term - terms, jnp.clip(moved + shift_b[term - terms], 0, n - 1)]

    def first_product(step, column):
        at = [place(step, column, which) for which in range(2)]
        slot = [slot_from(step, column, which) for which in range(2)]
        pair = jnp.concatenate(
            [
                jnp.where(live(slot[which]), states[at[which]].astype(jnp.float32), 0.0).astype(states.dtype)
                for which in range(2)
            ],
            axis=1,
        )
        for term in range(2 * terms):
            product = jnp.dot(lefts[term], pair, preferred_element_type=jnp.float32)
            for which in range(2):
                half[at[which], term] = (
                    product[:, which * size:(which + 1) * size] * weight(term, slot[which])
                ).astype(half.dtype)

    z_copy(0, 1).wait_recv()
    y_copy(0, 1).start()
    local[1].wait()
    for copy in others[:3]:
        copy.wait_recv()
    landed = [
        pltpu.make_async_copy(shift_in, shift_b, local_sem.at[3]),
        pltpu.make_async_copy(coef_in, coef_b, local_sem.at[4]),
    ]
    for copy in landed:
        copy.start()
    for copy in landed:
        copy.wait()
    first_product(0, 0)

    def gather(step, carry):
        for which in range(2):
            z_copy(step, which).wait_recv()
            y_copy(step, which).start()
        first_product(step, 0)
        for which in range(2):
            y_copy(step - 1, which).wait_recv()
        first_product(step - 1, 1)
        return carry

    repeat(1, depth, gather, 0)
    for which in range(2):
        y_copy(depth - 1, which).wait_recv()
    first_product(depth - 1, 1)
    local[2].wait()
    others[3].wait_recv()

    group = 4

    def second_product(row, column):
        labels = [slots[slot_of(row, column, which)] for which in range(2)]
        total = None
        for begin in range(0, 2 * terms, group):
            picked = []
            for which in range(2):
                tiles = []
                for term in range(begin, begin + group):
                    moved = shift[term] if term < terms else shift_b[term - terms]
                    tiles.append(half[inverse[labels[which] - moved + REACH], term])
                picked.append(jnp.concatenate(tiles, axis=1))
            product = jnp.dot(
                jnp.concatenate(picked, axis=0),
                rights[begin:begin + group].reshape(group * size, size),
                preferred_element_type=jnp.float32,
            )
            total = product if total is None else total + product
        return total[:size], total[size:]

    def part_copy(step, which):
        at = step * 2 + which
        return remote(part_out.at[at], part_in.at[at], part_send.at[at], part_recv.at[at], neighbour)

    def sum_copy(step, which):
        at = step * 2 + which
        return remote(
            sum_out.at[at], sum_in.at[at], sum_send.at[at], sum_recv.at[at], device(row_to(step), 0, which)
        )

    def scatter_y(step, carry):
        for which, part in enumerate(second_product(row_to(step), 1)):
            part_out[step * 2 + which] = part.astype(part_out.dtype)
            part_copy(step, which).start()
        return carry

    repeat(1, depth, scatter_y, 0)
    scatter_y(0, 0)

    def column_sum(step, which, part):
        part_copy(step, which).wait_recv()
        return part + part_in[step * 2 + which].astype(jnp.float32)

    def scatter_z(step, carry):
        for which, part in enumerate(second_product(row_to(step), 0)):
            sum_out[step * 2 + which] = column_sum(step, which, part).astype(sum_out.dtype)
            sum_copy(step, which).start()
        return carry

    repeat(1, depth, scatter_z, 0)
    parts = second_product(z, 0)
    sum_out[1] = column_sum(0, 1, parts[1]).astype(sum_out.dtype)
    sum_copy(0, 1).start()
    own = column_sum(0, 0, parts[0])

    def add_rows(which):
        def add(step, total):
            sum_copy(step, which).wait_recv()
            return total + sum_in[step * 2 + which].astype(jnp.float32)

        return add

    mine = live(me)
    out[0, core] = jnp.where(mine, repeat(1, depth, add_rows(0), own), 0.0).astype(out.dtype)
    sum_copy(0, 1).wait_recv()
    total = repeat(1, depth, add_rows(1), sum_in[1].astype(jnp.float32))
    out[0, 1 - core] = jnp.where(mine, total, 0.0).astype(out.dtype)

    for copy in others:
        copy.wait_send()
    z_copy(0, 1).wait_send()
    sum_copy(0, 1).wait_send()
    for which in range(2):
        y_copy(0, which).wait_send()
        part_copy(0, which).wait_send()

    def drain(step, carry):
        for which in range(2):
            z_copy(step, which).wait_send()
            y_copy(step, which).wait_send()
            part_copy(step, which).wait_send()
            sum_copy(step, which).wait_send()
        return carry

    repeat(1, depth, drain, 0)


def shards(n, wave, slots, rows, cols, left, right, coef, shift):
    terms, size = left.shape[0], left.shape[1]
    kept = wave.dtype
    smem = pl.BlockSpec(memory_space=pltpu.SMEM)
    anywhere = pl.BlockSpec(memory_space=pl.ANY)
    dma = pltpu.SemaphoreType.DMA
    return pl.pallas_call(
        functools.partial(sigma_kernel, n),
        out_shape=jax.ShapeDtypeStruct(wave.shape, kept),
        in_specs=[anywhere, smem, smem, smem, anywhere, anywhere, smem, smem, anywhere, anywhere],
        out_specs=pl.BlockSpec(memory_space=pltpu.VMEM),
        scratch_shapes=[
            pltpu.VMEM((2 * terms, size, size), kept),
            pltpu.VMEM((2 * terms, size, size), kept),
            pltpu.SMEM(coef.shape, coef.dtype),
            pltpu.SMEM(shift.shape, shift.dtype),
            pltpu.VMEM(coef.shape, coef.dtype),
            pltpu.VMEM(shift.shape, shift.dtype),
            pltpu.VMEM((n, size, size), kept),
            pltpu.VMEM((n + 1, 2 * terms, size, size), kept),
            pltpu.SMEM((n + 2 * REACH,), jnp.int32),
            pltpu.VMEM((n // 2, size, size), kept),
            pltpu.VMEM((n // 2, size, size), kept),
            pltpu.VMEM((n // 2, size, size), kept),
            pltpu.VMEM((n // 2, size, size), kept),
            dma((5,)), dma((4,)), dma((4,)),
            dma((n // 2,)), dma((n // 2,)), dma((n // 2,)), dma((n // 2,)),
            dma((n // 2,)), dma((n // 2,)), dma((n // 2,)), dma((n // 2,)),
        ],
        compiler_params=pltpu.CompilerParams(
            collective_id=0, has_side_effects=True, vmem_limit_bytes=56 * 1024 * 1024
        ),
    )(wave, slots, rows, cols, left, right, coef, shift, coef, shift)


def solution(mesh):
    return jax.shard_map(
        functools.partial(shards, mesh.shape["sec"]),
        mesh=mesh,
        in_specs=(
            P(("parts", "sec"), None, None, None),
            P("parts"),
            P("parts"),
            P("parts"),
            P(("parts", "sec"), None, None),
            P(("parts", "sec"), None, None),
            P(("parts", "sec"), None),
            P(("parts", "sec")),
        ),
        out_specs=P(("parts", "sec"), None, None, None),
        check_vma=False,
    )
```

```python
import functools

import jax
import jax.numpy as jnp
from jax import lax
from jax.experimental import pallas as pl
from jax.experimental.pallas import tpu as pltpu
from jax.sharding import PartitionSpec as P

MESH = pl.DeviceIdType.MESH
REACH = 2


def sigma_kernel(
    n, wave, slots, rows, cols, left, right, coef, shift, coef_far, shift_far,
    out,
    lefts, rights, coef_b, shift_b, coef_in, shift_in, states, half, inverse,
    part_out, part_in, sum_out, sum_in,
    local_sem, ops_send, ops_recv, z_send, z_recv, y_send, y_recv,
    part_send, part_recv, sum_send, sum_recv,
):
    depth = n // 4

    def repeat(begin, end, body, carry):
        if depth > 4:
            return lax.fori_loop(begin, end, body, carry)
        for step in range(begin, end):
            carry = body(step, carry)
        return carry

    terms = left.shape[0]
    size = wave.shape[2]
    me = lax.axis_index("sec")
    core = lax.rem(me, 2)
    y = lax.rem(me // 2, 2)
    z = me // 4

    def core_at(which):
        return 1 - core if which else core

    def row_to(step):
        return lax.rem(z + step, depth)

    def place(step, column, which):
        return (step * 2 + column) * 2 + which

    def slot_of(row, column, which):
        return (row * 2 + (1 - y if column else y)) * 2 + core_at(which)

    def slot_from(step, column, which):
        return slot_of(lax.rem(z + depth - step, depth), column, which)

    def device(row, column, which):
        return {"sec": slot_of(row, column, which)}

    def remote(src, dst, send, recv, target):
        return pltpu.make_async_remote_copy(
            src_ref=src, dst_ref=dst, send_sem=send, recv_sem=recv, device_id=target, device_id_type=MESH
        )

    local = [
        pltpu.make_async_copy(wave.at[0, core], states.at[0], local_sem.at[0]),
        pltpu.make_async_copy(left, lefts.at[pl.ds(0, terms)], local_sem.at[1]),
        pltpu.make_async_copy(right, rights.at[pl.ds(0, terms)], local_sem.at[2]),
    ]
    for copy in local:
        copy.start()

    barrier = pltpu.get_barrier_semaphore()

    def greet(step, carry):
        for which in range(2):
            pl.semaphore_signal(barrier, inc=1, device_id=device(row_to(step), 0, which), device_id_type=MESH)
        return carry

    partner = device(z, 0, 1)
    neighbour = device(z, 1, 0)
    pl.semaphore_signal(barrier, inc=1, device_id=partner, device_id_type=MESH)
    pl.semaphore_signal(barrier, inc=1, device_id=neighbour, device_id_type=MESH)
    repeat(1, depth, greet, 0)
    pl.semaphore_wait(barrier, 2 * depth)

    def z_copy(step, which):
        at = step * 2 + which
        return remote(
            wave.at[0, core_at(which)], states.at[place(step, 0, which)], z_send.at[at], z_recv.at[at],
            device(row_to(step), 0, which),
        )

    def y_copy(step, which):
        at = step * 2 + which
        return remote(
            states.at[place(step, 0, which)], states.at[place(step, 1, which)], y_send.at[at], y_recv.at[at],
            neighbour,
        )

    others = [
        remote(shift_far, shift_in, ops_send.at[0], ops_recv.at[0], partner),
        remote(coef_far, coef_in, ops_send.at[1], ops_recv.at[1], partner),
        remote(left, lefts.at[pl.ds(terms, terms)], ops_send.at[2], ops_recv.at[2], partner),
        remote(right, rights.at[pl.ds(terms, terms)], ops_send.at[3], ops_recv.at[3], partner),
    ]

    def send_column(step, carry):
        for which in range(2):
            z_copy(step, which).start()
        return carry

    repeat(1, depth, send_column, 0)
    z_copy(0, 1).start()
    for copy in others[:3]:
        copy.start()
    local[0].wait()
    y_copy(0, 0).start()
    others[3].start()

    for label in range(REACH):
        inverse[label] = n
        inverse[n + REACH + label] = n

    def slot_at(at):
        row = lax.rem(z + depth - at // 4, depth)
        column = lax.rem(y + lax.rem(at // 2, 2), 2)
        return (row * 2 + column) * 2 + lax.rem(core + lax.rem(at, 2), 2)

    if n > 16:
        def invert(label, carry):
            found = lax.fori_loop(
                0, n, lambda slot, seen: jnp.maximum(seen, jnp.where(slots[slot_at(slot)] == label, slot, 0)), jnp.int32(0)
            )
            inverse[label + REACH] = found
            return carry

        lax.fori_loop(0, n, invert, 0)
    else:
        names = []
        for at in range(n):
            step, rest = at // 4, at % 4
            names.append(slots[slot_from(step, rest // 2, rest % 2)])
        for label in range(n):
            found = jnp.int32(0)
            for at in range(1, n):
                found = jnp.where(names[at] == label, at, found)
            inverse[label + REACH] = found

    def clear(term, carry):
        half[n, term] = jnp.zeros((size, size), half.dtype)
        return carry

    lax.fori_loop(0, 2 * terms, clear, 0)

    row_of = lax.broadcasted_iota(jnp.int32, (size, size), 0)
    col_of = lax.broadcasted_iota(jnp.int32, (size, size), 1)

    def live(slot):
        label = slots[slot]
        return (row_of < rows[label]) & (col_of < cols[label])

    def weight(term, slot):
        moved = slots[slot]
        if term < terms:
            return coef[term, jnp.clip(moved + shift[term], 0, n - 1)]
        return coef_b[term - terms, jnp.clip(moved + shift_b[term - terms], 0, n - 1)]

    def first_product(step, column):
        at = [place(step, column, which) for which in range(2)]
        slot = [slot_from(step, column, which) for which in range(2)]
        pair = jnp.concatenate(
            [
                jnp.where(live(slot[which]), states[at[which]].astype(jnp.float32), 0.0).astype(states.dtype)
                for which in range(2)
            ],
            axis=1,
        )
        for term in range(2 * terms):
            product = jnp.dot(lefts[term], pair, preferred_element_type=jnp.float32)
            for which in range(2):
                half[at[which], term] = (
                    product[:, which * size:(which + 1) * size] * weight(term, slot[which])
                ).astype(half.dtype)

    z_copy(0, 1).wait_recv()
    y_copy(0, 1).start()
    local[1].wait()
    for copy in others[:3]:
        copy.wait_recv()
    landed = [
        pltpu.make_async_copy(shift_in, shift_b, local_sem.at[3]),
        pltpu.make_async_copy(coef_in, coef_b, local_sem.at[4]),
    ]
    for copy in landed:
        copy.start()
    for copy in landed:
        copy.wait()
    first_product(0, 0)

    def gather(step, carry):
        for which in range(2):
            z_copy(step, which).wait_recv()
            y_copy(step, which).start()
        first_product(step, 0)
        for which in range(2):
            y_copy(step - 1, which).wait_recv()
        first_product(step - 1, 1)
        return carry

    repeat(1, depth, gather, 0)
    for which in range(2):
        y_copy(depth - 1, which).wait_recv()
    first_product(depth - 1, 1)
    local[2].wait()
    others[3].wait_recv()

    group = 4

    def second_product(row, column):
        labels = [slots[slot_of(row, column, which)] for which in range(2)]
        total = None
        for begin in range(0, 2 * terms, group):
            picked = []
            for which in range(2):
                tiles = []
                for term in range(begin, begin + group):
                    moved = shift[term] if term < terms else shift_b[term - terms]
                    tiles.append(half[inverse[labels[which] - moved + REACH], term])
                picked.append(jnp.concatenate(tiles, axis=1))
            product = jnp.dot(
                jnp.concatenate(picked, axis=0),
                rights[begin:begin + group].reshape(group * size, size),
                preferred_element_type=jnp.float32,
            )
            total = product if total is None else total + product
        return total[:size], total[size:]

    def part_copy(step, which):
        at = step * 2 + which
        return remote(part_out.at[at], part_in.at[at], part_send.at[at], part_recv.at[at], neighbour)

    def sum_copy(step, which):
        at = step * 2 + which
        return remote(
            sum_out.at[at], sum_in.at[at], sum_send.at[at], sum_recv.at[at], device(row_to(step), 0, which)
        )

    def scatter_y(step, carry):
        for which, part in enumerate(second_product(row_to(step), 1)):
            part_out[step * 2 + which] = part.astype(part_out.dtype)
            part_copy(step, which).start()
        return carry

    repeat(1, depth, scatter_y, 0)
    scatter_y(0, 0)

    def column_sum(step, which, part):
        part_copy(step, which).wait_recv()
        return part + part_in[step * 2 + which].astype(jnp.float32)

    def scatter_z(step, carry):
        for which, part in enumerate(second_product(row_to(step), 0)):
            sum_out[step * 2 + which] = column_sum(step, which, part).astype(sum_out.dtype)
            sum_copy(step, which).start()
        return carry

    repeat(1, depth, scatter_z, 0)
    parts = second_product(z, 0)
    sum_out[1] = column_sum(0, 1, parts[1]).astype(sum_out.dtype)
    sum_copy(0, 1).start()
    own = column_sum(0, 0, parts[0])

    def add_rows(which):
        def add(step, total):
            sum_copy(step, which).wait_recv()
            return total + sum_in[step * 2 + which].astype(jnp.float32)

        return add

    mine = live(me)
    out[0, core] = jnp.where(mine, repeat(1, depth, add_rows(0), own), 0.0).astype(out.dtype)
    sum_copy(0, 1).wait_recv()
    total = repeat(1, depth, add_rows(1), sum_in[1].astype(jnp.float32))
    out[0, 1 - core] = jnp.where(mine, total, 0.0).astype(out.dtype)

    for copy in others:
        copy.wait_send()
    z_copy(0, 1).wait_send()
    sum_copy(0, 1).wait_send()
    for which in range(2):
        y_copy(0, which).wait_send()
        part_copy(0, which).wait_send()

    def drain(step, carry):
        for which in range(2):
            z_copy(step, which).wait_send()
            y_copy(step, which).wait_send()
            part_copy(step, which).wait_send()
            sum_copy(step, which).wait_send()
        return carry

    repeat(1, depth, drain, 0)


def shards(n, wave, slots, rows, cols, left, right, coef, shift):
    terms, size = left.shape[0], left.shape[1]
    kept = wave.dtype
    smem = pl.BlockSpec(memory_space=pltpu.SMEM)
    anywhere = pl.BlockSpec(memory_space=pl.ANY)
    dma = pltpu.SemaphoreType.DMA
    return pl.pallas_call(
        functools.partial(sigma_kernel, n),
        out_shape=jax.ShapeDtypeStruct(wave.shape, kept),
        in_specs=[anywhere, smem, smem, smem, anywhere, anywhere, smem, smem, anywhere, anywhere],
        out_specs=pl.BlockSpec(memory_space=pltpu.VMEM),
        scratch_shapes=[
            pltpu.VMEM((2 * terms, size, size), kept),
            pltpu.VMEM((2 * terms, size, size), kept),
            pltpu.SMEM(coef.shape, coef.dtype),
            pltpu.SMEM(shift.shape, shift.dtype),
            pltpu.VMEM(coef.shape, coef.dtype),
            pltpu.VMEM(shift.shape, shift.dtype),
            pltpu.VMEM((n, size, size), kept),
            pltpu.VMEM((n + 1, 2 * terms, size, size), kept),
            pltpu.SMEM((n + 2 * REACH,), jnp.int32),
            pltpu.VMEM((n // 2, size, size), kept),
            pltpu.VMEM((n // 2, size, size), kept),
            pltpu.VMEM((n // 2, size, size), kept),
            pltpu.VMEM((n // 2, size, size), kept),
            dma((5,)), dma((4,)), dma((4,)),
            dma((n // 2,)), dma((n // 2,)), dma((n // 2,)), dma((n // 2,)),
            dma((n // 2,)), dma((n // 2,)), dma((n // 2,)), dma((n // 2,)),
        ],
        compiler_params=pltpu.CompilerParams(
            collective_id=0, has_side_effects=True, vmem_limit_bytes=56 * 1024 * 1024
        ),
    )(wave, slots, rows, cols, left, right, coef, shift, coef, shift)


def solution(mesh):
    return jax.shard_map(
        functools.partial(shards, mesh.shape["sec"]),
        mesh=mesh,
        in_specs=(
            P(("parts", "sec"), None, None, None),
            P("parts"),
            P("parts"),
            P("parts"),
            P(("parts", "sec"), None, None),
            P(("parts", "sec"), None, None),
            P(("parts", "sec"), None),
            P(("parts", "sec")),
        ),
        out_specs=P(("parts", "sec"), None, None, None),
        check_vma=False,
    )
```
